32 devices in a mesh: groups: 2 (over x), stack: 4 (over y, core), bloch: 4 (over z).
Axes of the slice: x: 2, y: 2, z: 4, core: 2. Of those that a mesh axis runs over, the one named last changes fastest.
Arguments:
- drive: float32 [8, 8, 2, 192, 256], P(('groups', 'bloch'), 'stack'), parts along dimension 0, may hold values from -6 to 6
- positions: int32 [512], P('groups'), parts along dimension 0, may hold values from 0 to 3
- materials: int32 [16], P(('groups', 'stack')), parts along dimension 0, may hold values from 0 to 3
- table: float32 [4, 4, 192, 192], replicated, may hold values from -1 to 1
- thickness: float32 [16], P(('groups', 'stack')), parts along dimension 0, may hold values from 0.25 to 4
- decay: float32 [192], replicated, may hold values from 0.0025 to 2
Outputs:
- up_field: float32 [8, 4, 192, 256], P(('groups', 'bloch'), 'stack'), parts along dimension 0
- down_field: float32 [8, 4, 192, 256], P(('groups', 'bloch'), 'stack'), parts along dimension 0
The draws below stay inside these ranges and needn't reach their ends.
There are 2 independent parts, one for each index of `groups`. The reference program is written for one: setup_inputs(seed, part) draws one part's arguments, and reference() takes and returns one part's arrays. A program takes and returns all parts, laid end to end along the dimension named above; an argument that names none is the same for every part. Nothing has to cross between parts.
All inputs are finite; a program needn't handle non-finite values.
Results may differ from the reference program's by a relative error of at most 0.00013.
Values sent between devices are 32-bit elements; how exact they have to be, the bound alone decides.
A program may use at most 64 MiB of HBM per device.

```python
import math
import jax
import jax.numpy as jnp
from jax import lax

MODES = 192
COLS = 256
SLAB = 2
MATERIALS = 4
CELLS = 4
LAYERS = 8
SLABS = 4


def draw_table(key, part):
    key_refl = jax.random.fold_in(key, 11)
    key_couple = jax.random.fold_in(key, 23)
    key_diag = jax.random.fold_in(key, 37)
    couplings = jax.random.normal(key_couple, (MATERIALS, 2, MODES, MODES), jnp.float32) * (0.25 / math.sqrt(MODES))
    reflections = jax.random.normal(key_refl, (MATERIALS, 2, MODES, MODES), jnp.float32) * (0.3 / math.sqrt(MODES))
    diagonal = jax.random.uniform(key_diag, (MATERIALS, 2, MODES), jnp.float32, 0.7, 0.97)
    transmissions = couplings + diagonal[..., None] * jnp.eye(MODES, dtype=jnp.float32)
    blocks = jnp.stack([reflections[:, 0], transmissions[:, 0], transmissions[:, 1], reflections[:, 1]], axis=1)
    return jnp.clip(blocks, -1.0, 1.0)


def place_ends(entries, rng, smallest, top_value):
    extent = entries.shape
    spot = [jax.random.randint(jax.random.fold_in(rng, axis), (), 0, extent[axis]) for axis in range(len(extent))]
    entries = entries.at[tuple(spot)].set(smallest)
    longest = extent.index(max(extent))
    spot[longest] = (spot[longest] + 1) % extent[longest]
    return entries.at[tuple(spot)].set(top_value)


def levels(own_key, dims, split, low, top_value):
    def one(position, shards_of):
        draws = jax.random.uniform(jax.random.fold_in(jax.random.fold_in(own_key, 6), position), (shards_of,), jnp.float32, low / len(split), top_value / len(split))
        return jnp.repeat(jnp.exp(draws), dims[position] // shards_of).reshape((-1,) + (1,) * (len(dims) - position - 1))

    level = one(*split[0])
    for cut in split[1:]:
        level = level * one(*cut)
    return level


def normal_values(rng, extent, deviation, bound, pieces=(), kind=jnp.bfloat16):
    loudness = levels(rng, extent, pieces, -0.22, 0.18) if pieces else 1.0
    array = jax.random.normal(rng, extent, jnp.float32) * deviation * loudness
    return jnp.minimum(jnp.maximum(array, -bound), bound).astype(kind)


def setup_inputs(seed: int = 0, part: int = 0) -> dict:
    splits = jax.random.split(jax.random.key(seed), 7)
    part_splits = jax.random.split(jax.random.fold_in(splits[6], part), 7)
    return {
        "drive": normal_values(part_splits[0], (CELLS, LAYERS, 2, MODES, COLS), 1.0, 6.0, ((0, 4), (1, 4)), jnp.float32),
        "positions": place_ends(jax.random.randint(part_splits[1], (COLS,), 0, CELLS), jax.random.fold_in(part_splits[1], 1), 0, CELLS - 1).astype(jnp.int32),
        "materials": place_ends(jax.random.randint(part_splits[2], (LAYERS,), 0, MATERIALS), jax.random.fold_in(part_splits[2], 1), 0, MATERIALS - 1).astype(jnp.int32),
        "table": draw_table(jax.random.fold_in(splits[6], 71), part),
        "thickness": jnp.clip(jnp.exp(math.log(4.0) - 2.7725887 * jax.random.uniform(part_splits[4], (LAYERS,), jnp.float32) ** levels(part_splits[4], (LAYERS,), ((0, 4),), -0.2, 0.2)), 0.25, 4.0),
        "decay": jnp.clip(jnp.exp(jax.random.uniform(splits[5], (MODES,), jnp.float32, math.log(0.0025), math.log(2.0))), 0.0025, 2.0),
    }


precise = lax.Precision.HIGHEST

def product(left_side, right_side):
    return jnp.einsum('...ij,...jk->...ik', left_side, right_side, precision=precise)

def cas_table(cell_count):
    indices = jnp.arange(cell_count).astype(jnp.int32)
    phases = indices[:, None] * indices[None, :] % cell_count
    angles = phases.astype(jnp.float32) * (2.0 * math.pi / cell_count)
    return (jnp.cos(angles) + jnp.sin(angles)) / math.sqrt(cell_count)

def inverse_gap(coupling):
    identity = jnp.eye(coupling.shape[-1], dtype=coupling.dtype)
    system = identity - coupling
    return jnp.linalg.solve(system, jnp.broadcast_to(identity, system.shape))

def forward_join(above_part, below_part):
    refl_bot_a, src_down_a = above_part
    refl_top_b, trans_down_b, trans_up_b, refl_bot_b, src_up_b, src_down_b = below_part
    gap_inverse = inverse_gap(product(refl_bot_a, refl_top_b))
    down_inner = product(trans_down_b, gap_inverse)
    new_refl = refl_bot_b + product(down_inner, product(refl_bot_a, trans_up_b))
    new_source = src_down_b + product(down_inner, src_down_a + product(refl_bot_a, src_up_b))
    return (new_refl, new_source)

def backward_join(above_part, below_part):
    refl_top_a, trans_down_a, trans_up_a, refl_bot_a, src_up_a, src_down_a = above_part
    refl_top_b, src_up_b = below_part
    gap_inverse = inverse_gap(product(refl_bot_a, refl_top_b))
    reflect_inner = product(refl_top_b, gap_inverse)
    new_refl = refl_top_a + product(trans_up_a, product(reflect_inner, trans_down_a))
    crossing = product(gap_inverse, src_down_a + product(refl_bot_a, src_up_b))
    new_source = src_up_a + product(trans_up_a, product(refl_top_b, crossing) + src_up_b)
    return (new_refl, new_source)

def crossing_down(above_part, below_part):
    refl_bot_a, src_down_a = above_part
    refl_top_b, src_up_b = below_part
    gap_inverse = inverse_gap(product(refl_bot_a, refl_top_b))
    return product(gap_inverse, src_down_a + product(refl_bot_a, src_up_b))

def reference(drive, positions, materials, table, thickness, decay):
    cells = jnp.arange(CELLS).astype(jnp.int32)
    offset = jnp.abs(cells[:, None] - positions[None, :])
    offset = jnp.minimum(offset, CELLS - offset)
    envelope = 1.0 / (1.0 + offset.astype(jnp.float32))
    sources = drive * envelope[:, None, None, None, :]
    cas = cas_table(CELLS)
    spectrum = jnp.einsum('kc,clsme->klsme', cas, sources, precision=precise)
    waves = jnp.arange(CELLS).astype(jnp.float32)
    rates = decay[None, :] * (1.0 + 0.5 * jnp.cos(waves * (2.0 * math.pi / CELLS)))[:, None]
    chosen = table[materials]

    def element(layer_index):
        damping = jnp.exp(-thickness[layer_index] * rates)
        blocks = [damping[:, :, None] * chosen[layer_index, which][None] * damping[:, None, :] for which in range(4)]
        return (blocks[0], blocks[1], blocks[2], blocks[3], spectrum[:, layer_index, 0], spectrum[:, layer_index, 1])
    zero_matrix = jnp.zeros((CELLS, MODES, MODES), jnp.float32)
    zero_source = jnp.zeros((CELLS, MODES, COLS), jnp.float32)
    prefix = (zero_matrix, zero_source)
    tops = []
    bottoms = []
    for layer_index in range(LAYERS):
        if layer_index % SLAB == 0:
            tops.append(prefix)
        prefix = forward_join(prefix, element(layer_index))
        if layer_index % SLAB == SLAB - 1:
            bottoms.append(prefix)
    suffix = (zero_matrix, zero_source)
    below_list = [None] * SLABS
    from_list = [None] * SLABS
    for layer_index in range(LAYERS - 1, -1, -1):
        if layer_index % SLAB == SLAB - 1:
            below_list[layer_index // SLAB] = suffix
        suffix = backward_join(element(layer_index), suffix)
        if layer_index % SLAB == 0:
            from_list[layer_index // SLAB] = suffix
    up_list = []
    down_list = []
    for slab_index in range(SLABS):
        downward = crossing_down(tops[slab_index], from_list[slab_index])
        up_list.append(product(from_list[slab_index][0], downward) + from_list[slab_index][1])
        down_list.append(crossing_down(bottoms[slab_index], below_list[slab_index]))
    up_spec = jnp.stack(up_list, axis=1)
    down_spec = jnp.stack(down_list, axis=1)
    up_field = jnp.einsum('ck,ksme->csme', cas, up_spec, precision=precise)
    down_field = jnp.einsum('ck,ksme->csme', cas, down_spec, precision=precise)
    return (up_field, down_field)
```

```python
import functools
import math

import jax
import jax.numpy as jnp
from jax import lax
from jax.experimental import pallas as pl
from jax.experimental.pallas import tpu as pltpu
from jax.sharding import PartitionSpec as P

MESH = pl.DeviceIdType.MESH
f32 = jnp.float32
bf16 = jnp.bfloat16
R_IN, T_UP, GAP, D_DOWN, Q_BOT, R_D = range(6)


def split(value):
    high = value.astype(bf16)
    return high, (value - high.astype(f32)).astype(bf16)


def mm(left, right):
    return jnp.dot(left, right, preferred_element_type=f32)


def mm3(left, right):
    return mm(left[0], right[0]) + (mm(left[0], right[1]) + mm(left[1], right[0]))


def cas(row, column, count):
    angle = 2.0 * math.pi * (row * column % count) / count
    return (math.cos(angle) + math.sin(angle)) / math.sqrt(count)


def gap_series(couplings):
    rows = couplings[0].shape[0]
    splits = [split(c) for c in couplings]
    powers = [s[0] for s in splits]
    sums = list(couplings)
    squares = [mm(p, p) for p in powers]
    for step in range(5):
        powers = [s.astype(bf16) for s in squares]
        if step < 4:
            both = [
                mm(jnp.concatenate([e.astype(bf16), p], axis=0), p) for e, p in zip(sums, powers)
            ]
            sums = [e + s + b[:rows] for e, s, b in zip(sums, squares, both)]
            squares = [b[rows:] for b in both]
        else:
            last = [mm(e.astype(bf16), p) for e, p in zip(sums, powers)]
            sums = [e + s + b for e, s, b in zip(sums, squares, last)]
    parts = [split(e) for e in sums]
    rests = [c + mm3(cs, es) - e for c, cs, es, e in zip(couplings, splits, parts, sums)]
    return [e + r + mm(es[0], r.astype(bf16)) for e, r, es in zip(sums, rests, parts)]


def kernel(
    cells,
    depth,
    packed_ref,
    params_ref,
    table_ref,
    decay_row_ref,
    decay_col_ref,
    out_ref,
    params_all,
    drive_in,
    refl,
    held_high,
    held_low,
    u_send,
    u_in,
    x_send,
    x_in,
    field_send,
    field_in,
    params_sems,
    drive_sems,
    hop_sems,
    field_sems,
):
    slab_layers = packed_ref.shape[1]
    materials = table_ref.shape[0]
    lanes = packed_ref.shape[3]
    half = lanes // 2
    layers = depth * slab_layers
    slots = range(cells // 2 + 1)
    bloch = lax.axis_index("bloch")
    stack = lax.axis_index("stack")

    barrier = pltpu.get_barrier_semaphore()
    for j in range(1, cells):
        pl.semaphore_signal(
            barrier, inc=1, device_id={"bloch": lax.rem(bloch + j, cells)}, device_id_type=MESH
        )
    for j in range(1, depth):
        pl.semaphore_signal(
            barrier, inc=1, device_id={"stack": lax.rem(stack + j, depth)}, device_id_type=MESH
        )
    pl.semaphore_wait(barrier, cells + depth - 2)

    params_copies = []
    for j in range(1, depth):
        copy = pltpu.make_async_remote_copy(
            src_ref=params_ref,
            dst_ref=params_all.at[stack],
            send_sem=params_sems.at[0, j],
            recv_sem=params_sems.at[1, j],
            device_id={"stack": lax.rem(stack + j, depth)},
            device_id_type=MESH,
        )
        copy.start()
        params_copies.append(copy)
    drive_copies = []
    for j in range(1, cells):
        peer = lax.rem(bloch + j, cells)
        copy = pltpu.make_async_remote_copy(
            src_ref=packed_ref.at[peer],
            dst_ref=drive_in.at[bloch],
            send_sem=drive_sems.at[0, j],
            recv_sem=drive_sems.at[1, j],
            device_id={"bloch": peer},
            device_id_type=MESH,
        )
        copy.start()
        drive_copies.append(copy)
    params_all[stack] = params_ref[...]
    drive_in[bloch] = packed_ref[bloch]
    refl[...] = jnp.zeros_like(refl)
    for copy in params_copies:
        copy.wait()

    def hold(place, name, slot, value):
        parts = split(value)
        held_high[place, name, slot] = parts[0]
        held_low[place, name, slot] = parts[1]
        return parts

    def layer_step(turn, carry):
        layer = layers - 1 - turn
        place = lax.rem(layer, slab_layers)
        param = params_all[layer // slab_layers, place]
        width = param[0:1, :]
        chosen = []
        for block in range(4):
            total = None
            for n in range(materials):
                weight = jnp.where(param[1:2, :] == float(n), 1.0, 0.0)
                term = table_ref[n, block] * weight
                total = term if total is None else total + term
            chosen.append(total)
        row_rate = width * decay_row_ref[...]
        col_rate = width[:, 0:1] * decay_col_ref[...]
        scaled = []
        for slot in slots:
            factor = 1.0 + 0.5 * math.cos(2.0 * math.pi * slot / cells)
            row = jnp.exp(-row_rate * factor)
            col = jnp.exp(-col_rate * factor)
            scaled.append([col * block * row for block in chosen])
        below = [hold(place, R_IN, q, refl[q]) for q in slots]
        bottom = [hold(place, Q_BOT, q, scaled[q][3]) for q in slots]
        couplings = [mm3(below[q], bottom[q]) for q in slots]
        down = [hold(place, D_DOWN, q, scaled[q][1]) for q in slots]
        below_down = [hold(place, R_D, q, mm3(below[q], down[q])) for q in slots]
        gaps = gap_series(couplings)
        gap_parts = [hold(place, GAP, q, gaps[q]) for q in slots]
        ups = [split(scaled[q][2]) for q in slots]
        lifts = [
            hold(place, T_UP, q, scaled[q][2] + mm3(ups[q], gap_parts[q])) for q in slots
        ]
        for q in slots:
            refl[q] = scaled[q][0] + mm3(lifts[q], below_down[q])
        return carry

    lax.fori_loop(0, layers - slab_layers * stack, layer_step, 0)

    def held(place, name, slot):
        return held_high[place, name, slot], held_low[place, name, slot]

    def apply(place, name, values):
        return [mm3(held(place, name, q), split(values[q])) for q in slots]

    def added(*terms):
        return [functools.reduce(lambda a, b: a + b, group) for group in zip(*terms)]

    lift_all = [held(0, T_UP, q) for q in slots]
    for place in range(1, slab_layers):
        lift_all = [split(mm3(lift_all[q], held(place, T_UP, q))) for q in slots]
    through = None
    for place in range(slab_layers):
        bounce = []
        for q in slots:
            bottom = held(place, Q_BOT, q)
            whole = bottom[0].astype(f32) + bottom[1].astype(f32)
            bounce.append(split(whole + mm3(bottom, held(place, GAP, q))))
        step = []
        for q in slots:
            down = held(place, D_DOWN, q)
            whole = down[0].astype(f32) + down[1].astype(f32)
            step.append(split(whole + mm3(bounce[q], held(place, R_D, q))))
        through = step if through is None else [split(mm3(step[q], through[q])) for q in slots]

    for copy in drive_copies:
        copy.wait()
    lane = lax.broadcasted_iota(jnp.int32, drive_in.shape[2:], 1)
    lower = lane < half
    up_src, down_src = [], []
    for place in range(slab_layers):
        spectrum = []
        for k in range(cells):
            total = None
            for c in range(cells):
                term = drive_in[c, place] * cas(k, c, cells)
                total = term if total is None else total + term
            spectrum.append(total)
        ups, downs = [], []
        for q in slots:
            one, other = spectrum[q], spectrum[(cells - q) % cells]
            ups.append(jnp.where(lower, one, pltpu.roll(other, half, 1)))
            downs.append(jnp.where(lower, pltpu.roll(one, half, 1), other))
        up_src.append(ups)
        down_src.append(downs)

    lit = [apply(place, R_IN, down_src[place]) for place in range(slab_layers)]
    base = None
    for place in reversed(range(slab_layers)):
        inner = lit[place] if base is None else added(lit[place], base)
        base = added(up_src[place], apply(place, T_UP, inner))

    def hop(send_ref, in_ref, which, peer):
        return pltpu.make_async_remote_copy(
            src_ref=send_ref,
            dst_ref=in_ref,
            send_sem=hop_sems.at[0, which],
            recv_sem=hop_sems.at[1, which],
            device_id={"stack": peer},
            device_id_type=MESH,
        )

    hop_up = hop(u_send, u_in, 0, lax.rem(stack + depth - 1, depth))
    hop_down = hop(x_send, x_in, 1, lax.rem(stack + 1, depth))

    @pl.when(stack == depth - 1)
    def _():
        u_in[...] = jnp.zeros_like(u_in)

    @pl.when(stack < depth - 1)
    def _():
        hop_up.wait_recv()

    under = [u_in[q] for q in slots]
    top = added(base, [mm3(lift_all[q], split(under[q])) for q in slots])
    for q in slots:
        u_send[q] = top[q]

    @pl.when(stack > 0)
    def _():
        hop_up.start()

    inner_up = [under]
    for place in reversed(range(1, slab_layers)):
        inner = added(lit[place], inner_up[0])
        inner_up.insert(0, added(up_src[place], apply(place, T_UP, inner)))
    falling = None
    for place in range(slab_layers):
        gone = down_src[place]
        if falling is not None:
            gone = added(gone, apply(place, D_DOWN, falling))
            rise = added(apply(place, R_IN, gone), inner_up[place])
        else:
            rise = added(lit[place], inner_up[place])
        rise = added(rise, apply(place, GAP, rise))
        falling = added(gone, apply(place, Q_BOT, rise))

    @pl.when(stack == 0)
    def _():
        x_in[...] = jnp.zeros_like(x_in)

    @pl.when(stack > 0)
    def _():
        hop_down.wait_recv()

    over = [split(x_in[q]) for q in slots]
    lowest = added(falling, [mm3(through[q], over[q]) for q in slots])
    for q in slots:
        x_send[q] = lowest[q]

    @pl.when(stack < depth - 1)
    def _():
        hop_down.start()

    highest = added(top, [mm3(split(refl[q]), over[q]) for q in slots])
    for c in range(cells):
        rise, fall = None, None
        for q in slots:
            other = (cells - q) % cells
            other_weight = cas(c, other, cells) if other != q else 0.0
            weight = jnp.where(lower, cas(c, q, cells), other_weight)
            rise = highest[q] * weight if rise is None else rise + highest[q] * weight
            fall = lowest[q] * weight if fall is None else fall + lowest[q] * weight
        rise = rise + pltpu.roll(rise, half, 1)
        fall = fall + pltpu.roll(fall, half, 1)
        field_send[c] = jnp.where(lower, rise, fall)
    field_copies = []
    for j in range(1, cells):
        peer = lax.rem(bloch + j, cells)
        copy = pltpu.make_async_remote_copy(
            src_ref=field_send.at[peer],
            dst_ref=field_in.at[bloch],
            send_sem=field_sems.at[0, j],
            recv_sem=field_sems.at[1, j],
            device_id={"bloch": peer},
            device_id_type=MESH,
        )
        copy.start()
        field_copies.append(copy)
    field_in[bloch] = field_send[bloch]

    @pl.when(stack > 0)
    def _():
        hop_up.wait_send()

    @pl.when(stack < depth - 1)
    def _():
        hop_down.wait_send()

    for copy in field_copies:
        copy.wait()
    out_ref[...] = field_in[...]


def shards(drive, positions, materials, table, thickness, decay):
    cells_here, slab_layers, ways, modes, columns = drive.shape
    cells = cells_here * lax.axis_size("bloch")
    depth = lax.axis_size("stack")
    assert cells_here == 1 and ways == 2
    share = columns // cells
    half = max(share, 64)
    offset = jnp.abs(lax.axis_index("bloch") - positions)
    offset = jnp.minimum(offset, cells - offset)
    envelope = 1.0 / (1.0 + offset.astype(f32))
    sources = drive[0] * envelope
    packed = sources.reshape(slab_layers, ways, modes, cells, share)
    packed = jnp.transpose(packed, (3, 0, 2, 1, 4))
    packed = jnp.pad(packed, ((0, 0),) * 4 + ((0, half - share),))
    packed = packed.reshape(cells, slab_layers, modes, ways * half)
    params = jnp.stack([thickness] + [materials.astype(f32)] * 7, axis=1)
    params = jnp.broadcast_to(params[:, :, None], (slab_layers, 8, modes))
    slots = cells // 2 + 1
    lanes = ways * half
    vmem = pl.BlockSpec(memory_space=pltpu.VMEM)
    fields = pl.pallas_call(
        functools.partial(kernel, cells, depth),
        out_shape=jax.ShapeDtypeStruct((cells, modes, lanes), f32),
        in_specs=[vmem] * 5,
        out_specs=vmem,
        scratch_shapes=[
            pltpu.VMEM((depth, slab_layers, 8, modes), f32),
            pltpu.VMEM((cells, slab_layers, modes, lanes), f32),
            pltpu.VMEM((slots, modes, modes), f32),
            pltpu.VMEM((slab_layers, 6, slots, modes, modes), bf16),
            pltpu.VMEM((slab_layers, 6, slots, modes, modes), bf16),
            pltpu.VMEM((slots, modes, lanes), f32),
            pltpu.VMEM((slots, modes, lanes), f32),
            pltpu.VMEM((slots, modes, lanes), f32),
            pltpu.VMEM((slots, modes, lanes), f32),
            pltpu.VMEM((cells, modes, lanes), f32),
            pltpu.VMEM((cells, modes, lanes), f32),
            pltpu.SemaphoreType.DMA((2, depth)),
            pltpu.SemaphoreType.DMA((2, cells)),
            pltpu.SemaphoreType.DMA((2, 2)),
            pltpu.SemaphoreType.DMA((2, cells)),
        ],
        compiler_params=pltpu.CompilerParams(
            collective_id=0, has_side_effects=True, vmem_limit_bytes=48 * 1024 * 1024
        ),
    )(packed, params, table, decay[None, :], decay[:, None])
    fields = fields.reshape(cells, modes, ways, half)[..., :share]
    fields = jnp.transpose(fields, (2, 1, 0, 3)).reshape(ways, 1, 1, modes, columns)
    return (fields[0], fields[1])


def solution(mesh):
    in_specs = (
        P(("groups", "bloch"), "stack", None, None, None),
        P("groups"),
        P(("groups", "stack")),
        P(),
        P(("groups", "stack")),
        P(),
    )
    out_specs = (
        P(("groups", "bloch"), "stack", None, None),
        P(("groups", "bloch"), "stack", None, None),
    )
    return jax.shard_map(shards, mesh=mesh, in_specs=in_specs, out_specs=out_specs, check_vma=False)
```

```python
import functools
import math

import jax
import jax.numpy as jnp
from jax import lax
from jax.experimental import pallas as pl
from jax.experimental.pallas import tpu as pltpu
from jax.sharding import PartitionSpec as P

MESH = pl.DeviceIdType.MESH
f32 = jnp.float32
bf16 = jnp.bfloat16
R_IN, T_UP, GAP, D_DOWN, Q_BOT, R_D = range(6)


def split(value):
    high = value.astype(bf16)
    return high, (value - high.astype(f32)).astype(bf16)


def stacked(value):
    return jnp.concatenate(split(value), axis=0)


def mm(left, right):
    return jnp.dot(left, right, preferred_element_type=f32)


def mm3(left, right):
    rows, inner = left.shape[0] // 2, right.shape[0] // 2
    both = mm(left, right[:inner])
    return both[:rows] + (both[rows:] + mm(left[:rows], right[inner:]))


def mm3_columns(left, columns):
    rows, lanes = left.shape[0] // 2, columns.shape[1]
    both = mm(left, jnp.concatenate(split(columns), axis=1))
    cross = both[:rows, lanes:] + both[rows:, :lanes] + both[rows:, lanes:]
    return both[:rows, :lanes] + cross


def cas(row, column, count):
    angle = 2.0 * math.pi * (row * column % count) / count
    return (math.cos(angle) + math.sin(angle)) / math.sqrt(count)


def gap_series(couplings):
    rows = couplings[0].shape[0]
    splits = [stacked(c) for c in couplings]
    powers = [s[:rows] for s in splits]
    sums = list(couplings)
    squares = [mm(p, p) for p in powers]
    for step in range(5):
        powers = [s.astype(bf16) for s in squares]
        if step < 4:
            both = [
                mm(jnp.concatenate([e.astype(bf16), p], axis=0), p) for e, p in zip(sums, powers)
            ]
            sums = [e + s + b[:rows] for e, s, b in zip(sums, squares, both)]
            squares = [b[rows:] for b in both]
        else:
            last = [mm(e.astype(bf16), p) for e, p in zip(sums, powers)]
            sums = [e + s + b for e, s, b in zip(sums, squares, last)]
    parts = [stacked(e) for e in sums]
    rests = [c + mm3(cs, es) - e for c, cs, es, e in zip(couplings, splits, parts, sums)]
    return [e + r + mm(es[:rows], r.astype(bf16)) for e, r, es in zip(sums, rests, parts)]


def kernel(
    cells,
    depth,
    drive_hbm,
    positions_ref,
    thickness_ref,
    materials_ref,
    table_hbm,
    decay_row_ref,
    up_ref,
    down_ref,
    drive_ref,
    table_ref,
    packed_ref,
    params_ref,
    params_all,
    drive_in,
    refl,
    held,
    through,
    u_send,
    u_in,
    x_send,
    x_in,
    field_send,
    field_in,
    load_sems,
    params_sems,
    drive_sems,
    hop_sems,
    field_sems,
):
    slab_layers = packed_ref.shape[1]
    materials = table_ref.shape[0]
    modes = packed_ref.shape[2]
    lanes = packed_ref.shape[3]
    half = lanes // 2
    share = drive_ref.shape[-1] // cells
    layers = depth * slab_layers
    slots = range(cells // 2 + 1)
    groups = range(cells // 2)
    pairs = [(0, cells // 2)] + [(g, cells - g) for g in groups if g > 0]
    bloch = lax.axis_index("bloch")
    stack = lax.axis_index("stack")
    drive_copy = pltpu.make_async_copy(drive_hbm, drive_ref, load_sems.at[0])
    drive_copy.start()
    table_copy = pltpu.make_async_copy(table_hbm, table_ref, load_sems.at[1])
    table_copy.start()

    barrier = pltpu.get_barrier_semaphore()
    for j in range(1, cells):
        pl.semaphore_signal(
            barrier, inc=1, device_id={"bloch": lax.rem(bloch + j, cells)}, device_id_type=MESH
        )
    for j in range(1, depth):
        pl.semaphore_signal(
            barrier, inc=1, device_id={"stack": lax.rem(stack + j, depth)}, device_id_type=MESH
        )
    param_row = lax.broadcasted_iota(jnp.int32, params_ref.shape[1:], 0)
    for place in range(slab_layers):
        material = materials_ref[place].astype(f32)
        params_ref[place] = jnp.where(param_row == 0, thickness_ref[place], material)
    decay_col = jnp.transpose(jnp.broadcast_to(decay_row_ref[...], (128, modes)))[:, 0:1]
    drive_copy.wait()
    offset = jnp.abs(bloch - positions_ref[...])
    offset = jnp.minimum(offset, cells - offset)
    envelope = 1.0 / (1.0 + offset.astype(f32))
    for place in range(slab_layers):
        ways = [drive_ref[0, place, way] * envelope for way in range(2)]
        for c in range(cells):
            pieces = []
            for way in ways:
                pieces.append(way[:, c * share : (c + 1) * share])
                if share < half:
                    pieces.append(jnp.zeros((modes, half - share), f32))
            packed_ref[c, place] = jnp.concatenate(pieces, axis=1)
    pl.semaphore_wait(barrier, cells + depth - 2)

    params_copies = []
    for j in range(1, depth):
        copy = pltpu.make_async_remote_copy(
            src_ref=params_ref,
            dst_ref=params_all.at[stack],
            send_sem=params_sems.at[0, j],
            recv_sem=params_sems.at[1, j],
            device_id={"stack": lax.rem(stack + j, depth)},
            device_id_type=MESH,
        )
        copy.start()
        params_copies.append(copy)
    drive_copies = []
    for j in range(1, cells):
        peer = lax.rem(bloch + j, cells)
        copy = pltpu.make_async_remote_copy(
            src_ref=packed_ref.at[peer],
            dst_ref=drive_in.at[bloch],
            send_sem=drive_sems.at[0, j],
            recv_sem=drive_sems.at[1, j],
            device_id={"bloch": peer},
            device_id_type=MESH,
        )
        copy.start()
        drive_copies.append(copy)
    params_all[stack] = params_ref[...]
    drive_in[bloch] = packed_ref[bloch]
    refl[...] = jnp.zeros_like(refl)
    table_copy.wait()
    for copy in params_copies:
        copy.wait()

    def hold(place, name, slot, value):
        parts = stacked(value)
        held[place, name, slot] = parts
        return parts

    def layer_blocks(turn):
        layer = layers - 1 - turn
        place = lax.rem(layer, slab_layers)
        param = params_all[layer // slab_layers, place]
        width = param[0:1, :]
        chosen = []
        for block in range(4):
            total = None
            for n in range(materials):
                weight = jnp.where(param[1:2, :] == float(n), 1.0, 0.0)
                term = table_ref[n, block] * weight
                total = term if total is None else total + term
            chosen.append(total)
        row_rate = width * decay_row_ref[...]
        col_rate = width[:, 0:1] * decay_col
        scaled = []
        for slot in slots:
            factor = 1.0 + 0.5 * math.cos(2.0 * math.pi * slot / cells)
            row = jnp.exp(-row_rate * factor)
            col = jnp.exp(-col_rate * factor)
            scaled.append([col * block * row for block in chosen])
        down = [hold(place, D_DOWN, q, scaled[q][1]) for q in slots]
        bottom = [hold(place, Q_BOT, q, scaled[q][3]) for q in slots]

        return place, scaled, down, bottom

    place, scaled, down, bottom = layer_blocks(0)
    for q in slots:
        empty = jnp.zeros((2 * modes, modes), bf16)
        held[place, R_IN, q] = empty
        held[place, R_D, q] = empty
        held[place, GAP, q] = empty
        hold(place, T_UP, q, scaled[q][2])
        refl[q] = scaled[q][0]

    def layer_step(turn, carry):
        place, scaled, down, bottom = layer_blocks(turn)
        below = [hold(place, R_IN, q, refl[q]) for q in slots]
        couplings = [mm3(below[q], bottom[q]) for q in slots]
        below_down = [hold(place, R_D, q, mm3(below[q], down[q])) for q in slots]
        gaps = gap_series(couplings)
        gap_parts = [hold(place, GAP, q, gaps[q]) for q in slots]
        ups = [stacked(scaled[q][2]) for q in slots]
        lifts = [hold(place, T_UP, q, scaled[q][2] + mm3(ups[q], gap_parts[q])) for q in slots]
        for q in slots:
            refl[q] = scaled[q][0] + mm3(lifts[q], below_down[q])
        return carry

    lax.fori_loop(1, layers - slab_layers * stack, layer_step, 0)

    lane = lax.broadcasted_iota(jnp.int32, (modes, lanes), 1)
    lower = lane < half

    def act(matrix, group, columns):
        if group > 0:
            return mm3_columns(matrix(group), columns)
        one = mm3_columns(matrix(0), columns)
        return jnp.where(lower, one, mm3_columns(matrix(cells // 2), columns))

    def apply(place, name, values):
        return [act(lambda q: held[place, name, q], g, values[g]) for g in groups]

    def added(*terms):
        return [functools.reduce(lambda a, b: a + b, group) for group in zip(*terms)]

    lift_all = [held[0, T_UP, q] for q in slots]
    for place in range(1, slab_layers):
        lift_all = [stacked(mm3(lift_all[q], held[place, T_UP, q])) for q in slots]

    def whole(place, name, q):
        return held[place, name, q, :modes].astype(f32) + held[place, name, q, modes:].astype(f32)

    @pl.when(stack > 0)
    def _():
        total = None
        for place in range(slab_layers):
            bounce = [
                stacked(whole(place, Q_BOT, q) + mm3(held[place, Q_BOT, q], held[place, GAP, q]))
                for q in slots
            ]
            step = [
                stacked(whole(place, D_DOWN, q) + mm3(bounce[q], held[place, R_D, q]))
                for q in slots
            ]
            total = step if total is None else [stacked(mm3(step[q], total[q])) for q in slots]
        for q in slots:
            through[q] = total[q]

    for copy in drive_copies:
        copy.wait()
    up_src, down_src = [], []
    for place in range(slab_layers):
        spectrum = []
        for k in range(cells):
            total = None
            for c in range(cells):
                term = drive_in[c, place] * cas(k, c, cells)
                total = term if total is None else total + term
            spectrum.append(total)
        ups, downs = [], []
        for first, second in pairs:
            one, other = spectrum[first], spectrum[second]
            ups.append(jnp.where(lower, one, pltpu.roll(other, half, 1)))
            downs.append(jnp.where(lower, pltpu.roll(one, half, 1), other))
        up_src.append(ups)
        down_src.append(downs)

    lit = [apply(place, R_IN, down_src[place]) for place in range(slab_layers)]
    base = None
    for place in reversed(range(slab_layers)):
        inner = lit[place] if base is None else added(lit[place], base)
        base = added(up_src[place], apply(place, T_UP, inner))

    def hop(send_ref, in_ref, which, peer):
        return [
            pltpu.make_async_remote_copy(
                src_ref=send_ref.at[g],
                dst_ref=in_ref.at[g],
                send_sem=hop_sems.at[0, which, g],
                recv_sem=hop_sems.at[1, which, g],
                device_id={"stack": peer},
                device_id_type=MESH,
            )
            for g in groups
        ]

    hop_up = hop(u_send, u_in, 0, lax.rem(stack + depth - 1, depth))
    hop_down = hop(x_send, x_in, 1, lax.rem(stack + 1, depth))

    @pl.when(stack == depth - 1)
    def _():
        u_in[...] = jnp.zeros_like(u_in)

    under, top = [], []
    for g in groups:

        @pl.when(stack < depth - 1)
        def _():
            hop_up[g].wait_recv()

        under.append(u_in[g])
        top.append(base[g] + act(lambda q: lift_all[q], g, under[g]))
        u_send[g] = top[g]

        @pl.when(stack > 0)
        def _():
            hop_up[g].start()

    inner_up = [under]
    for place in reversed(range(1, slab_layers)):
        inner = added(lit[place], inner_up[0])
        inner_up.insert(0, added(up_src[place], apply(place, T_UP, inner)))
    falling = None
    for place in range(slab_layers):
        gone = down_src[place]
        if falling is not None:
            gone = added(gone, apply(place, D_DOWN, falling))
            rise = added(apply(place, R_IN, gone), inner_up[place])
        else:
            rise = added(lit[place], inner_up[place])
        rise = added(rise, apply(place, GAP, rise))
        falling = added(gone, apply(place, Q_BOT, rise))

    @pl.when(stack == 0)
    def _():
        x_in[...] = jnp.zeros_like(x_in)

    lowest = []
    for g in groups:
        x_send[g] = falling[g]

        @pl.when(stack > 0)
        def _():
            hop_down[g].wait_recv()
            x_send[g] = falling[g] + act(lambda q: through[q], g, x_in[g])

        @pl.when(stack < depth - 1)
        def _():
            hop_down[g].start()

        lowest.append(x_send[g])

    refl_parts = [stacked(refl[q]) for q in slots]
    highest = [top[g] + act(lambda q: refl_parts[q], g, x_in[g]) for g in groups]
    for c in range(cells):
        rise, fall = None, None
        for g in groups:
            weight = jnp.where(lower, cas(c, pairs[g][0], cells), cas(c, pairs[g][1], cells))
            rise = highest[g] * weight if rise is None else rise + highest[g] * weight
            fall = lowest[g] * weight if fall is None else fall + lowest[g] * weight
        rise = rise + pltpu.roll(rise, half, 1)
        fall = fall + pltpu.roll(fall, half, 1)
        field_send[c] = jnp.where(lower, rise, fall)
    field_copies = []
    for j in range(1, cells):
        peer = lax.rem(bloch + j, cells)
        copy = pltpu.make_async_remote_copy(
            src_ref=field_send.at[peer],
            dst_ref=field_in.at[bloch],
            send_sem=field_sems.at[0, j],
            recv_sem=field_sems.at[1, j],
            device_id={"bloch": peer},
            device_id_type=MESH,
        )
        copy.start()
        field_copies.append(copy)
    field_in[bloch] = field_send[bloch]

    @pl.when(stack > 0)
    def _():
        for copy in hop_up:
            copy.wait_send()

    @pl.when(stack < depth - 1)
    def _():
        for copy in hop_down:
            copy.wait_send()

    for copy in field_copies:
        copy.wait()
    up_ref[0, 0] = jnp.concatenate([field_in[c, :, :share] for c in range(cells)], axis=1)
    down_ref[0, 0] = jnp.concatenate(
        [field_in[c, :, half : half + share] for c in range(cells)], axis=1
    )


def shards(drive, positions, materials, table, thickness, decay):
    cells_here, slab_layers, ways, modes, columns = drive.shape
    cells = cells_here * lax.axis_size("bloch")
    depth = lax.axis_size("stack")
    assert cells_here == 1 and ways == 2
    share = columns // cells
    half = max(share, 64)
    slots = cells // 2 + 1
    lanes = ways * half
    vmem = pl.BlockSpec(memory_space=pltpu.VMEM)
    smem = pl.BlockSpec(memory_space=pltpu.SMEM)
    anywhere = pl.BlockSpec(memory_space=pl.ANY)
    hop_buffer = pltpu.VMEM((cells // 2, modes, lanes), f32)
    cell_buffer = pltpu.VMEM((cells, modes, lanes), f32)
    field = jax.ShapeDtypeStruct((1, 1, modes, columns), f32)
    up_field, down_field = pl.pallas_call(
        functools.partial(kernel, cells, depth),
        out_shape=(field, field),
        in_specs=[anywhere, vmem, smem, smem, anywhere, vmem],
        out_specs=(vmem, vmem),
        scratch_shapes=[
            pltpu.VMEM(drive.shape, f32),
            pltpu.VMEM(table.shape, f32),
            pltpu.VMEM((cells, slab_layers, modes, lanes), f32),
            pltpu.VMEM((slab_layers, 8, modes), f32),
            pltpu.VMEM((depth, slab_layers, 8, modes), f32),
            pltpu.VMEM((cells, slab_layers, modes, lanes), f32),
            pltpu.VMEM((slots, modes, modes), f32),
            pltpu.VMEM((slab_layers, 6, slots, 2 * modes, modes), bf16),
            pltpu.VMEM((slots, 2 * modes, modes), bf16),
            hop_buffer,
            hop_buffer,
            hop_buffer,
            hop_buffer,
            cell_buffer,
            cell_buffer,
            pltpu.SemaphoreType.DMA((2,)),
            pltpu.SemaphoreType.DMA((2, depth)),
            pltpu.SemaphoreType.DMA((2, cells)),
            pltpu.SemaphoreType.DMA((2, 2, cells // 2)),
            pltpu.SemaphoreType.DMA((2, cells)),
        ],
        compiler_params=pltpu.CompilerParams(
            collective_id=0, has_side_effects=True, vmem_limit_bytes=60 * 1024 * 1024
        ),
    )(drive, positions[None, :], thickness, materials, table, decay[None, :])
    return (up_field, down_field)


def solution(mesh):
    in_specs = (
        P(("groups", "bloch"), "stack", None, None, None),
        P("groups"),
        P(("groups", "stack")),
        P(),
        P(("groups", "stack")),
        P(),
    )
    out_specs = (
        P(("groups", "bloch"), "stack", None, None),
        P(("groups", "bloch"), "stack", None, None),
    )
    return jax.shard_map(shards, mesh=mesh, in_specs=in_specs, out_specs=out_specs, check_vma=False)
```

```python
import functools
import math

import jax
import jax.numpy as jnp
from jax import lax
from jax.experimental import pallas as pl
from jax.experimental.pallas import tpu as pltpu
from jax.sharding import PartitionSpec as P

MESH = pl.DeviceIdType.MESH
f32 = jnp.float32
bf16 = jnp.bfloat16
R_IN, T_UP, GAP, D_DOWN, Q_BOT, R_D = range(6)


def split(value):
    high = value.astype(bf16)
    return high, (value - high.astype(f32)).astype(bf16)


def stacked(value):
    return jnp.concatenate(split(value), axis=0)


def mm(left, right):
    return jnp.dot(left, right, preferred_element_type=f32)


def mm3(left, right):
    rows, inner = left.shape[0] // 2, right.shape[0] // 2
    both = mm(left, right[:inner])
    return both[:rows] + (both[rows:] + mm(left[:rows], right[inner:]))


def mm3_columns(left, columns):
    rows, lanes = left.shape[0] // 2, columns.shape[1]
    both = mm(left, jnp.concatenate(split(columns), axis=1))
    cross = both[:rows, lanes:] + both[rows:, :lanes] + both[rows:, lanes:]
    return both[:rows, :lanes] + cross


def cas(row, column, count):
    angle = 2.0 * math.pi * (row * column % count) / count
    return (math.cos(angle) + math.sin(angle)) / math.sqrt(count)


def gap_series(couplings):
    rows = couplings[0].shape[0]
    splits = [stacked(c) for c in couplings]
    powers = [s[:rows] for s in splits]
    sums = list(couplings)
    squares = [mm(p, p) for p in powers]
    for step in range(5):
        powers = [s.astype(bf16) for s in squares]
        if step < 4:
            both = [
                mm(jnp.concatenate([e.astype(bf16), p], axis=0), p) for e, p in zip(sums, powers)
            ]
            sums = [e + s + b[:rows] for e, s, b in zip(sums, squares, both)]
            squares = [b[rows:] for b in both]
        else:
            last = [mm(e.astype(bf16), p) for e, p in zip(sums, powers)]
            sums = [e + s + b for e, s, b in zip(sums, squares, last)]
    parts = [stacked(e) for e in sums]
    rests = [c + mm3(cs, es) - e for c, cs, es, e in zip(couplings, splits, parts, sums)]
    return [e + r + mm(es[:rows], r.astype(bf16)) for e, r, es in zip(sums, rests, parts)]


def kernel(
    cells,
    depth,
    drive_hbm,
    positions_ref,
    thickness_ref,
    materials_ref,
    table_hbm,
    decay_row_ref,
    up_ref,
    down_ref,
    drive_ref,
    table_ref,
    packed_ref,
    params_ref,
    params_all,
    drive_in,
    refl,
    held,
    through,
    u_send,
    u_in,
    x_send,
    x_in,
    field_send,
    field_in,
    load_sems,
    params_sems,
    drive_sems,
    hop_sems,
    field_sems,
):
    slab_layers = packed_ref.shape[1]
    materials = table_ref.shape[0]
    modes = packed_ref.shape[2]
    lanes = packed_ref.shape[3]
    half = lanes // 2
    share = drive_ref.shape[-1] // cells
    layers = depth * slab_layers
    slots = range(cells // 2 + 1)
    groups = range(cells // 2)
    pairs = [(0, cells // 2)] + [(g, cells - g) for g in groups if g > 0]
    bloch = lax.axis_index("bloch")
    stack = lax.axis_index("stack")
    drive_copy = pltpu.make_async_copy(drive_hbm, drive_ref, load_sems.at[0])
    drive_copy.start()
    table_copy = pltpu.make_async_copy(table_hbm, table_ref, load_sems.at[1])
    table_copy.start()

    barrier = pltpu.get_barrier_semaphore()
    for j in range(1, cells):
        pl.semaphore_signal(
            barrier, inc=1, device_id={"bloch": lax.rem(bloch + j, cells)}, device_id_type=MESH
        )
    for j in range(1, depth):
        pl.semaphore_signal(
            barrier, inc=1, device_id={"stack": lax.rem(stack + j, depth)}, device_id_type=MESH
        )
    param_row = lax.broadcasted_iota(jnp.int32, params_ref.shape[1:], 0)
    for place in range(slab_layers):
        material = materials_ref[place].astype(f32)
        params_ref[place] = jnp.where(param_row == 0, thickness_ref[place], material)
    decay_col = jnp.transpose(jnp.broadcast_to(decay_row_ref[...], (128, modes)))[:, 0:1]
    drive_copy.wait()
    offset = jnp.abs(bloch - positions_ref[...])
    offset = jnp.minimum(offset, cells - offset)
    envelope = 1.0 / (1.0 + offset.astype(f32))
    for place in range(slab_layers):
        ways = [drive_ref[0, place, way] * envelope for way in range(2)]
        for c in range(cells):
            pieces = []
            for way in ways:
                pieces.append(way[:, c * share : (c + 1) * share])
                if share < half:
                    pieces.append(jnp.zeros((modes, half - share), f32))
            packed_ref[c, place] = jnp.concatenate(pieces, axis=1)
    pl.semaphore_wait(barrier, cells + depth - 2)

    params_copies = []
    for j in range(1, depth):
        copy = pltpu.make_async_remote_copy(
            src_ref=params_ref,
            dst_ref=params_all.at[stack],
            send_sem=params_sems.at[0, j],
            recv_sem=params_sems.at[1, j],
            device_id={"stack": lax.rem(stack + j, depth)},
            device_id_type=MESH,
        )
        copy.start()
        params_copies.append(copy)
    drive_copies = []
    for j in range(1, cells):
        peer = lax.rem(bloch + j, cells)
        copy = pltpu.make_async_remote_copy(
            src_ref=packed_ref.at[peer],
            dst_ref=drive_in.at[bloch],
            send_sem=drive_sems.at[0, j],
            recv_sem=drive_sems.at[1, j],
            device_id={"bloch": peer},
            device_id_type=MESH,
        )
        copy.start()
        drive_copies.append(copy)
    params_all[stack] = params_ref[...]
    drive_in[bloch] = packed_ref[bloch]
    refl[...] = jnp.zeros_like(refl)
    table_copy.wait()
    for copy in params_copies:
        copy.wait()

    def hold(place, name, slot, value):
        parts = stacked(value)
        held[place, name, slot] = parts
        return parts

    def layer_blocks(turn):
        layer = layers - 1 - turn
        place = lax.rem(layer, slab_layers)
        param = params_all[layer // slab_layers, place]
        width = param[0:1, :]
        chosen = []
        material = jnp.broadcast_to(param[1:2, :], (modes, modes))
        for block in range(4):
            total = table_ref[0, block]
            for n in range(1, materials):
                total = jnp.where(material == float(n), table_ref[n, block], total)
            chosen.append(total)
        row_rate = width * decay_row_ref[...]
        col_rate = width[:, 0:1] * decay_col
        scaled = []
        for slot in slots:
            factor = 1.0 + 0.5 * math.cos(2.0 * math.pi * slot / cells)
            row = jnp.exp(-row_rate * factor)
            col = jnp.exp(-col_rate * factor)
            scaled.append([col * block * row for block in chosen])
        down = [hold(place, D_DOWN, q, scaled[q][1]) for q in slots]
        bottom = [hold(place, Q_BOT, q, scaled[q][3]) for q in slots]

        return place, scaled, down, bottom

    place, scaled, down, bottom = layer_blocks(0)
    for q in slots:
        empty = jnp.zeros((2 * modes, modes), bf16)
        held[place, R_IN, q] = empty
        held[place, R_D, q] = empty
        held[place, GAP, q] = empty
        hold(place, T_UP, q, scaled[q][2])
        refl[q] = scaled[q][0]

    def layer_step(turn, carry):
        place, scaled, down, bottom = layer_blocks(turn)
        below = [hold(place, R_IN, q, refl[q]) for q in slots]
        couplings = [mm3(below[q], bottom[q]) for q in slots]
        below_down = [hold(place, R_D, q, mm3(below[q], down[q])) for q in slots]
        gaps = gap_series(couplings)
        gap_parts = [hold(place, GAP, q, gaps[q]) for q in slots]
        ups = [stacked(scaled[q][2]) for q in slots]
        lifts = [hold(place, T_UP, q, scaled[q][2] + mm3(ups[q], gap_parts[q])) for q in slots]
        for q in slots:
            refl[q] = scaled[q][0] + mm3(lifts[q], below_down[q])
        return carry

    lax.fori_loop(1, layers - slab_layers * stack, layer_step, 0)

    lane = lax.broadcasted_iota(jnp.int32, (modes, lanes), 1)
    lower = lane < half

    def act(matrix, group, columns):
        if group > 0:
            return mm3_columns(matrix(group), columns)
        one = mm3_columns(matrix(0), columns)
        return jnp.where(lower, one, mm3_columns(matrix(cells // 2), columns))

    def apply(place, name, values):
        return [act(lambda q: held[place, name, q], g, values[g]) for g in groups]

    def added(*terms):
        return [functools.reduce(lambda a, b: a + b, group) for group in zip(*terms)]

    lift_all = [held[0, T_UP, q] for q in slots]
    for place in range(1, slab_layers):
        lift_all = [stacked(mm3(lift_all[q], held[place, T_UP, q])) for q in slots]

    def whole(place, name, q):
        return held[place, name, q, :modes].astype(f32) + held[place, name, q, modes:].astype(f32)

    @pl.when(stack > 0)
    def _():
        total = None
        for place in range(slab_layers):
            bounce = [
                stacked(whole(place, Q_BOT, q) + mm3(held[place, Q_BOT, q], held[place, GAP, q]))
                for q in slots
            ]
            step = [
                stacked(whole(place, D_DOWN, q) + mm3(bounce[q], held[place, R_D, q]))
                for q in slots
            ]
            total = step if total is None else [stacked(mm3(step[q], total[q])) for q in slots]
        for q in slots:
            through[q] = total[q]

    for copy in drive_copies:
        copy.wait()
    up_src, down_src = [], []
    for place in range(slab_layers):
        spectrum = []
        for k in range(cells):
            total = None
            for c in range(cells):
                term = drive_in[c, place] * cas(k, c, cells)
                total = term if total is None else total + term
            spectrum.append(total)
        ups, downs = [], []
        for first, second in pairs:
            one, other = spectrum[first], spectrum[second]
            ups.append(jnp.where(lower, one, pltpu.roll(other, half, 1)))
            downs.append(jnp.where(lower, pltpu.roll(one, half, 1), other))
        up_src.append(ups)
        down_src.append(downs)

    lit = [apply(place, R_IN, down_src[place]) for place in range(slab_layers)]
    base = None
    for place in reversed(range(slab_layers)):
        inner = lit[place] if base is None else added(lit[place], base)
        base = added(up_src[place], apply(place, T_UP, inner))

    def hop(send_ref, in_ref, which, peer):
        return [
            pltpu.make_async_remote_copy(
                src_ref=send_ref.at[g],
                dst_ref=in_ref.at[g],
                send_sem=hop_sems.at[0, which, g],
                recv_sem=hop_sems.at[1, which, g],
                device_id={"stack": peer},
                device_id_type=MESH,
            )
            for g in groups
        ]

    hop_up = hop(u_send, u_in, 0, lax.rem(stack + depth - 1, depth))
    hop_down = hop(x_send, x_in, 1, lax.rem(stack + 1, depth))

    @pl.when(stack == depth - 1)
    def _():
        u_in[...] = jnp.zeros_like(u_in)

    under, top = [], []
    for g in groups:

        @pl.when(stack < depth - 1)
        def _():
            hop_up[g].wait_recv()

        under.append(u_in[g])
        top.append(base[g] + act(lambda q: lift_all[q], g, under[g]))
        u_send[g] = top[g]

        @pl.when(stack > 0)
        def _():
            hop_up[g].start()

    inner_up = [under]
    for place in reversed(range(1, slab_layers)):
        inner = added(lit[place], inner_up[0])
        inner_up.insert(0, added(up_src[place], apply(place, T_UP, inner)))
    falling = None
    for place in range(slab_layers):
        gone = down_src[place]
        if falling is not None:
            gone = added(gone, apply(place, D_DOWN, falling))
            rise = added(apply(place, R_IN, gone), inner_up[place])
        else:
            rise = added(lit[place], inner_up[place])
        rise = added(rise, apply(place, GAP, rise))
        falling = added(gone, apply(place, Q_BOT, rise))

    @pl.when(stack == 0)
    def _():
        x_in[...] = jnp.zeros_like(x_in)

    lowest = []
    for g in groups:
        x_send[g] = falling[g]

        @pl.when(stack > 0)
        def _():
            hop_down[g].wait_recv()
            x_send[g] = falling[g] + act(lambda q: through[q], g, x_in[g])

        @pl.when(stack < depth - 1)
        def _():
            hop_down[g].start()

        lowest.append(x_send[g])

    refl_parts = [stacked(refl[q]) for q in slots]
    highest = [top[g] + act(lambda q: refl_parts[q], g, x_in[g]) for g in groups]
    for c in range(cells):
        rise, fall = None, None
        for g in groups:
            weight = jnp.where(lower, cas(c, pairs[g][0], cells), cas(c, pairs[g][1], cells))
            rise = highest[g] * weight if rise is None else rise + highest[g] * weight
            fall = lowest[g] * weight if fall is None else fall + lowest[g] * weight
        rise = rise + pltpu.roll(rise, half, 1)
        fall = fall + pltpu.roll(fall, half, 1)
        field_send[c] = jnp.where(lower, rise, fall)
    field_copies = []
    for j in range(1, cells):
        peer = lax.rem(bloch + j, cells)
        copy = pltpu.make_async_remote_copy(
            src_ref=field_send.at[peer],
            dst_ref=field_in.at[bloch],
            send_sem=field_sems.at[0, j],
            recv_sem=field_sems.at[1, j],
            device_id={"bloch": peer},
            device_id_type=MESH,
        )
        copy.start()
        field_copies.append(copy)
    field_in[bloch] = field_send[bloch]

    @pl.when(stack > 0)
    def _():
        for copy in hop_up:
            copy.wait_send()

    @pl.when(stack < depth - 1)
    def _():
        for copy in hop_down:
            copy.wait_send()

    for copy in field_copies:
        copy.wait()
    up_ref[0, 0] = jnp.concatenate([field_in[c, :, :share] for c in range(cells)], axis=1)
    down_ref[0, 0] = jnp.concatenate(
        [field_in[c, :, half : half + share] for c in range(cells)], axis=1
    )


def shards(drive, positions, materials, table, thickness, decay):
    cells_here, slab_layers, ways, modes, columns = drive.shape
    cells = cells_here * lax.axis_size("bloch")
    depth = lax.axis_size("stack")
    assert cells_here == 1 and ways == 2
    share = columns // cells
    half = max(share, 64)
    slots = cells // 2 + 1
    lanes = ways * half
    vmem = pl.BlockSpec(memory_space=pltpu.VMEM)
    smem = pl.BlockSpec(memory_space=pltpu.SMEM)
    anywhere = pl.BlockSpec(memory_space=pl.ANY)
    hop_buffer = pltpu.VMEM((cells // 2, modes, lanes), f32)
    cell_buffer = pltpu.VMEM((cells, modes, lanes), f32)
    field = jax.ShapeDtypeStruct((1, 1, modes, columns), f32)
    up_field, down_field = pl.pallas_call(
        functools.partial(kernel, cells, depth),
        out_shape=(field, field),
        in_specs=[anywhere, vmem, smem, smem, anywhere, vmem],
        out_specs=(vmem, vmem),
        scratch_shapes=[
            pltpu.VMEM(drive.shape, f32),
            pltpu.VMEM(table.shape, f32),
            pltpu.VMEM((cells, slab_layers, modes, lanes), f32),
            pltpu.VMEM((slab_layers, 8, modes), f32),
            pltpu.VMEM((depth, slab_layers, 8, modes), f32),
            pltpu.VMEM((cells, slab_layers, modes, lanes), f32),
            pltpu.VMEM((slots, modes, modes), f32),
            pltpu.VMEM((slab_layers, 6, slots, 2 * modes, modes), bf16),
            pltpu.VMEM((slots, 2 * modes, modes), bf16),
            hop_buffer,
            hop_buffer,
            hop_buffer,
            hop_buffer,
            cell_buffer,
            cell_buffer,
            pltpu.SemaphoreType.DMA((2,)),
            pltpu.SemaphoreType.DMA((2, depth)),
            pltpu.SemaphoreType.DMA((2, cells)),
            pltpu.SemaphoreType.DMA((2, 2, cells // 2)),
            pltpu.SemaphoreType.DMA((2, cells)),
        ],
        compiler_params=pltpu.CompilerParams(
            collective_id=0, has_side_effects=True, vmem_limit_bytes=60 * 1024 * 1024
        ),
    )(drive, positions[None, :], thickness, materials, table, decay[None, :])
    return (up_field, down_field)


def solution(mesh):
    in_specs = (
        P(("groups", "bloch"), "stack", None, None, None),
        P("groups"),
        P(("groups", "stack")),
        P(),
        P(("groups", "stack")),
        P(),
    )
    out_specs = (
        P(("groups", "bloch"), "stack", None, None),
        P(("groups", "bloch"), "stack", None, None),
    )
    return jax.shard_map(shards, mesh=mesh, in_specs=in_specs, out_specs=out_specs, check_vma=False)
```
